256 devices in a mesh: tile: 64 (over z, y, core), frame: 4 (over x).
Axes of the slice: x: 4, y: 4, z: 8, core: 2. Of those that a mesh axis runs over, the one named last changes fastest.
Arguments:
- movie: bfloat16 [1572864, 512], P('tile', 'frame'), may hold values from -150 to 150
- footprint: float32 [12288, 8, 128], P('tile'), may hold values from 0 to 1, as said below
- traces: float32 [12288, 512], P('tile', 'frame'), may hold values from 0.05 to 3
- slot_neuron: int32 [12288, 8], P('tile'), may hold values from 0 to 12288, as said below
- neuron_blocks: int32 [12288, 8], P('tile'), may hold values from 0 to 98304, as said below
Outputs:
- footprint_new: float32 [12288, 8, 128], P('tile', None, 'frame')
- traces_new: float32 [12288, 512], P('tile', 'frame')
The draws below stay inside these ranges and needn't reach their ends.
Inputs may be any that keep to these rules, and one draw needn't show every extreme that they name: `slot_neuron`: entry 12288 marks an empty slot. Neuron n sits in exactly the slots that row n of neuron_blocks lists, at most once in a voxel block. `neuron_blocks`: row n lists the slot indices (voxel block * 8 + slot) of neuron n: 1 to 8 consecutive voxel blocks in one slot, in increasing order, then the pad 12288 * 8. Neuron n has its home at tile index n // 192 and lies wholly in tile (n // 192 + n) mod 64. The blocks of one home tile index's neurons in one tile number at most 24, and some pair of home and tile reaches 24. `footprint`: zero in empty slots.
All inputs are finite; a program needn't handle non-finite values.
Results may differ from the reference program's by a relative error of at most 0.0054.
Values may be sent and summed in bfloat16 or wider, within the bound.
No kernel may reach another device: no remote copies, remote signals or barrier semaphores. Data moves between devices by JAX's collectives and lax.ppermute only.
A program may use at most 64 MiB of HBM per device.

```python
import jax
import jax.numpy as jnp
from jax import lax

BLOCK = 128
BLKS_T = 192
NEUR_DEV = 192
SLOTS = 8
KB = 8
NEUR = 12288
VBLOCKS = 12288
VOX = 1572864
FRAMES = 512
N_TILE = 64


def layout(key):
    positions = NEUR_DEV // SLOTS
    stride = BLKS_T // positions
    neuron = jnp.arange(NEUR)
    home_tile = neuron // NEUR_DEV
    local_index = neuron % NEUR_DEV
    tile_index = (home_tile + local_index) % N_TILE
    within = local_index // N_TILE * N_TILE + home_tile
    subkeys = jax.random.split(jax.random.fold_in(key, 11), N_TILE)
    orders = jax.vmap(lambda subkey: jax.random.permutation(subkey, NEUR_DEV))(subkeys)
    placed = orders[tile_index, within]
    slot_layer = placed % SLOTS
    position = placed // SLOTS
    counts = jax.random.randint(jax.random.fold_in(key, 12), (NEUR,), 1, KB + 1)
    chosen = jax.random.randint(jax.random.fold_in(key, 13), (2,), 0, N_TILE)
    counts = jnp.where((home_tile == chosen[0]) & (tile_index == chosen[1]), KB, counts)
    jitter = jax.random.randint(jax.random.fold_in(key, 14), (NEUR,), 0, stride - counts + 1)
    first_block = position * stride + jitter
    offsets = jnp.arange(KB)
    filled = offsets[None, :] < counts[:, None]
    global_slot = (tile_index[:, None] * BLKS_T + first_block[:, None] + offsets[None, :]) * SLOTS + slot_layer[:, None]
    padding = VBLOCKS * SLOTS
    neuron_blocks = jnp.where(filled, global_slot, padding).astype(jnp.int32)
    owners = jnp.repeat(neuron, KB).astype(jnp.int32)
    slot_neuron = jnp.full((padding,), NEUR, jnp.int32).at[neuron_blocks.reshape(-1)].set(owners, mode='drop')
    return (slot_neuron.reshape(VBLOCKS, SLOTS), neuron_blocks)


def draw_slot_neuron(key, part):
    return layout(key)[0]


def draw_neuron_blocks(key, part):
    return layout(key)[1]


def draw_footprint(key, part):
    occupied = (layout(key)[0] < NEUR).astype(jnp.float32)
    key = jax.random.fold_in(key, 3)
    key_values, key_scales = jax.random.split(key)
    values = jax.random.uniform(key_values, (VBLOCKS, SLOTS, BLOCK))
    scales = jnp.exp(jax.random.uniform(key_scales, (VBLOCKS, SLOTS, 1), minval=jnp.log(0.2), maxval=0.0))
    return (values * scales * occupied[..., None]).astype(jnp.float32)


def draw_traces(key, part):
    key = jax.random.fold_in(key, 5)
    key_values = jax.random.fold_in(key, 0)
    values = jax.random.uniform(key_values, (NEUR, FRAMES), minval=jnp.log(0.05), maxval=jnp.log(3.0))
    return jnp.exp(values).astype(jnp.float32)


def level_of(rng, extent, cuts, least, top_value):
    def one(dim, parts):
        draws = jax.random.uniform(jax.random.fold_in(jax.random.fold_in(rng, 6), dim), (parts,), jnp.float32, least / len(cuts), top_value / len(cuts))
        return jnp.repeat(jnp.exp(draws), extent[dim] // parts).reshape((-1,) + (1,) * (len(extent) - dim - 1))

    loudness = one(*cuts[0])
    for cut in cuts[1:]:
        loudness = loudness * one(*cut)
    return loudness


def bell_draw(own_key, shape, deviation, limit, pieces=(), kind=jnp.bfloat16):
    loudness = level_of(own_key, shape, pieces, -0.22, 0.18) if pieces else 1.0
    drawn = jax.random.normal(own_key, shape, jnp.float32) * deviation * loudness
    return jnp.minimum(jnp.maximum(drawn, -limit), limit).astype(kind)


def setup_inputs(seed: int = 0) -> dict:
    streams_of = jax.random.split(jax.random.key(seed), 6)
    return {
        "movie": bell_draw(streams_of[0], (VOX, FRAMES), 25.0, 150.0, ((0, 64), (1, 4))),
        "footprint": draw_footprint(jax.random.fold_in(streams_of[5], 71), 0),
        "traces": draw_traces(jax.random.fold_in(streams_of[5], 71), 0),
        "slot_neuron": draw_slot_neuron(jax.random.fold_in(streams_of[5], 71), 0),
        "neuron_blocks": draw_neuron_blocks(jax.random.fold_in(streams_of[5], 71), 0),
    }


sparsity = 50.0
highest = lax.Precision.HIGHEST


def tile_update(inputs):
    movie_cube, slot_rows, footprint, occupied = inputs
    movie_wide = movie_cube.astype(jnp.float32)
    rows_wide = slot_rows.astype(jnp.float32)
    correlation = jnp.einsum("ovf,osf->osv", movie_wide, rows_wide, precision=highest)
    gram_block = jnp.einsum("osf,otf->ost", rows_wide, rows_wide, precision=highest)
    diagonal = jnp.diagonal(gram_block, axis1=1, axis2=2)
    divisor = jnp.where(occupied, diagonal, 1.0)
    mixed_term = jnp.einsum("ots,otv->osv", gram_block, footprint, precision=highest)
    updated = jnp.maximum(footprint + (correlation - mixed_term - sparsity) / divisor[..., None], 0.0)
    updated = jnp.where(occupied[..., None], updated, 0.0)
    footprint_low = updated.astype(jnp.bfloat16)
    projected = jnp.einsum("osv,ovf->osf", footprint_low.astype(jnp.float32), movie_wide, precision=highest)
    cross_norm = jnp.einsum("osv,otv->ost", updated, updated, precision=highest)
    slot_grad = projected - jnp.einsum("ost,otf->osf", cross_norm, rows_wide, precision=highest)
    slot_norm = jnp.diagonal(cross_norm, axis1=1, axis2=2)
    return updated, slot_grad, slot_norm


def reference(movie, footprint, traces, slot_neuron, neuron_blocks):
    traces_low = traces.astype(jnp.bfloat16)
    flat_lists = neuron_blocks.reshape(-1).astype(jnp.int32)
    source = jnp.repeat(traces_low, KB, axis=0)
    slot_rows = jnp.zeros((VBLOCKS * SLOTS, FRAMES), jnp.bfloat16).at[flat_lists].set(source, mode="drop")
    occupied = slot_neuron < NEUR
    movie_cube = movie.reshape(N_TILE, BLKS_T, BLOCK, FRAMES)
    rows_tiles = slot_rows.reshape(N_TILE, BLKS_T, SLOTS, FRAMES)
    foot_tiles = footprint.reshape(N_TILE, BLKS_T, SLOTS, BLOCK)
    live_tiles = occupied.reshape(N_TILE, BLKS_T, SLOTS)
    updated, slot_grad, slot_norm = lax.map(tile_update, (movie_cube, rows_tiles, foot_tiles, live_tiles))
    grad_flat = jnp.concatenate([slot_grad.reshape(-1, FRAMES), jnp.zeros((1, FRAMES), slot_grad.dtype)], 0)
    norm_flat = jnp.concatenate([slot_norm.reshape(-1), jnp.zeros((1,), slot_norm.dtype)], 0)
    trace_grad = grad_flat[flat_lists].reshape(NEUR, KB, FRAMES).sum(1)
    weight = norm_flat[flat_lists].reshape(NEUR, KB).sum(1)
    traces_new = jnp.maximum(traces + trace_grad / jnp.maximum(weight, 1.0)[:, None], 0.0)
    return updated.reshape(VBLOCKS, SLOTS, BLOCK), traces_new
```

```python
import jax
import jax.numpy as jnp
from jax import lax
from jax.experimental import pallas as pl
from jax.experimental.pallas import tpu as pltpu
from jax.sharding import PartitionSpec as P

sparsity = 50.0
lane = 128
f32, bf16 = jnp.float32, jnp.bfloat16
nn = (((1,), (0,)), ((), ()))
nt = (((1,), (1,)), ((), ()))


def dot(a, b, dims=nn):
    return lax.dot_general(a, b, dims, preferred_element_type=f32)


def halves(x):
    high = x.astype(bf16)
    return high, (x - high.astype(f32)).astype(bf16)


def masks():
    row = lax.broadcasted_iota(jnp.int32, (lane, lane), 0)
    col = lax.broadcasted_iota(jnp.int32, (lane, lane), 1)
    return row == col, (row // 8) == (col // 8)


def column(eye, row):
    return jnp.sum(jnp.where(eye, row, 0.0), axis=1, keepdims=True)


def first_kernel(
    groups, recv, id_row, owner, foot_hbm, movie_hbm, rows_out, send, movie, foot, diag, packed, sem_m, sem_f, sem_o
):
    voxels = movie.shape[0] // groups

    def movie_copy(g):
        at = pl.ds(g * voxels, voxels)
        return pltpu.make_async_copy(movie_hbm.at[at], movie.at[at], sem_m.at[g])

    def foot_copy(g):
        at = pl.ds(g * lane, lane)
        return pltpu.make_async_copy(foot_hbm.at[at], foot.at[at], sem_f.at[g])

    for g in range(groups):
        foot_copy(g).start()
        movie_copy(g).start()
    eye, block = masks()
    diag[...] = jnp.zeros_like(diag)

    def body(g, carry):
        at = pl.ds(pl.multiple_of(g * lane, lane), lane)
        own = column(eye, owner[pl.ds(g, 1), :].astype(f32))
        onehot = (own == id_row[...]).astype(bf16)
        rows = dot(onehot, recv[...]).astype(bf16)
        rows_out[at, :] = rows
        gram = jnp.where(block, dot(rows, rows, nt), 0.0)
        diag[pl.ds(g, 1), :] = jnp.sum(jnp.where(eye, gram, 0.0), axis=0, keepdims=True)
        foot_copy(g).wait()
        gh, gl = halves(gram)
        fh, fl = halves(foot[at, :])
        mixed = dot(gh, fh) + dot(gl, fh) + dot(gh, fl)
        movie_copy(g).wait()
        for p in range(8):
            two = pl.ds(pl.multiple_of(g * voxels + p * 256, 256), 256)
            both = dot(rows[16 * p : 16 * p + 16], movie[two, :], nt)
            corr = jnp.concatenate([both[:8, :lane], both[8:, lane:]], 0)
            packed[pl.ds(pl.multiple_of(g * lane + p * 16, 16), 16), :] = (
                corr - mixed[16 * p : 16 * p + 16]
            ).astype(bf16)
        return carry

    lax.fori_loop(0, groups, body, 0)
    dh, dl = halves(diag[...])
    packed[pl.ds(groups * lane, 16), :] = dh
    packed[pl.ds(groups * lane + 16, 16), :] = dl
    for k in range(send.shape[0]):
        pltpu.make_async_copy(packed, send.at[k], sem_o.at[k]).start()
    for k in range(send.shape[0]):
        pltpu.make_async_copy(packed, send.at[k], sem_o.at[k]).wait()


def second_kernel(
    groups, total_neurons, quarter, got, rows_in, owner, id_col, foot_hbm, movie_hbm, kept, ratio, movie, foot, acc, wacc, inv, sem_m, sem_f
):
    voxels = movie.shape[0] // groups
    shares = got.shape[0]
    width = kept.shape[1]

    def movie_copy(g):
        at = pl.ds(g * voxels, voxels)
        return pltpu.make_async_copy(movie_hbm.at[at], movie.at[at], sem_m.at[g])

    def foot_copy(g):
        at = pl.ds(g * lane, lane)
        return pltpu.make_async_copy(foot_hbm.at[at], foot.at[at], sem_f.at[g])

    for g in range(groups):
        foot_copy(g).start()
        movie_copy(g).start()
    eye, block = masks()
    acc[...] = jnp.zeros_like(acc)
    wacc[...] = jnp.zeros_like(wacc)
    total = jnp.zeros((16, lane), f32)
    for k in range(shares):
        total += got[k, pl.ds(groups * lane, 16), :].astype(f32)
        total += got[k, pl.ds(groups * lane + 16, 16), :].astype(f32)
    inv[...] = total
    low_rows = lax.broadcasted_iota(jnp.int32, (16, lane), 0) < 8
    shift = lax.rem(lane - quarter[0] * width, lane)

    def body(g, carry):
        at = pl.ds(pl.multiple_of(g * lane, lane), lane)
        own = owner[pl.ds(g, 1), :]
        live = column(eye, (own < total_neurons).astype(f32)) > 0.0
        divisor = jnp.where(live, column(eye, inv[pl.ds(g, 1), :]), 1.0)
        residual = got[0, at, :].astype(f32)
        for k in range(1, shares):
            residual += got[k, at, :].astype(f32)
        foot_copy(g).wait()
        updated = jnp.maximum(foot[at, :] + (residual - sparsity) / divisor, 0.0)
        updated = jnp.where(live, updated, 0.0)
        kept[at, :] = pltpu.roll(updated, shift, 1)[:, :width]
        uh, ul = halves(updated)
        cross = dot(uh, uh, nt) + dot(uh, ul, nt) + dot(ul, uh, nt)
        cross = jnp.where(block, cross, 0.0)
        rows = rows_in[at, :]
        ch, cl = halves(cross)
        known = dot(ch, rows) + dot(cl, rows)
        movie_copy(g).wait()
        parts = []
        for p in range(8):
            two = pl.ds(pl.multiple_of(g * voxels + p * 256, 256), 256)
            part = updated[16 * p : 16 * p + 16]
            wide = jnp.concatenate([jnp.where(low_rows, part, 0.0), jnp.where(low_rows, 0.0, part)], 1)
            parts.append(dot(wide.astype(bf16), movie[two, :]))
        grad = jnp.concatenate(parts, 0) - known
        picks = own == id_col[...]
        onehot = picks.astype(bf16)
        hi, lo = halves(grad)
        acc[...] += dot(onehot, hi) + dot(onehot, lo)
        norm = jnp.sum(jnp.where(eye, cross, 0.0), axis=0, keepdims=True)
        wacc[...] += jnp.where(picks, norm, 0.0)
        return carry

    lax.fori_loop(0, groups, body, 0)
    weight = jnp.sum(wacc[...], axis=1, keepdims=True)
    ratio[...] = acc[...] / jnp.maximum(weight, 1.0)


def local(movie, footprint, traces, slot_neuron, neuron_blocks):
    tiles, shares = lax.axis_size("tile"), lax.axis_size("frame")
    blocks, slots, width = footprint.shape
    homes, frames = traces.shape
    per_pair = homes // tiles
    slot_total = blocks * slots
    groups = slot_total // lane
    tile = lax.axis_index("tile")
    frame = lax.axis_index("frame")

    low = traces.astype(bf16).reshape(per_pair, tiles, frames).transpose(1, 0, 2)
    low = jnp.pad(low, ((0, 0), (0, 4 - per_pair), (0, 0)))
    twice = jnp.concatenate([low, low], 0)
    leaving = lax.dynamic_slice_in_dim(twice, lax.rem(tiles - tile, tiles), tiles, 0)
    recv = lax.all_to_all(leaving, "tile", 0, 0).reshape(4 * tiles, frames)

    k = jnp.arange(4 * tiles, dtype=jnp.int32)
    home, j = k // 4, k % 4
    ids = jnp.where(j < per_pair, homes * home + tiles * j + (tile + tiles - home) % tiles, -1)
    owner = slot_neuron.reshape(groups, lane)
    foot = footprint.reshape(slot_total, width)

    anywhere = pl.BlockSpec(memory_space=pl.ANY)
    vmem = pl.BlockSpec(memory_space=pltpu.VMEM)
    params = pltpu.CompilerParams(vmem_limit_bytes=40 * 1024 * 1024)
    tall = slot_total + 32

    def call(kernel, *static, **kw):
        return pl.pallas_call(lambda *refs: kernel(groups, *static, *refs), compiler_params=params, **kw)

    rows, send = call(
        first_kernel,
        out_shape=(
            jax.ShapeDtypeStruct((slot_total, frames), bf16),
            jax.ShapeDtypeStruct((shares, tall, width), bf16),
        ),
        in_specs=[vmem, vmem, vmem, anywhere, anywhere],
        out_specs=(vmem, anywhere),
        scratch_shapes=[
            pltpu.VMEM(movie.shape, bf16),
            pltpu.VMEM((slot_total, width), f32),
            pltpu.VMEM((16, lane), f32),
            pltpu.VMEM((tall, width), bf16),
            pltpu.SemaphoreType.DMA((groups,)),
            pltpu.SemaphoreType.DMA((groups,)),
            pltpu.SemaphoreType.DMA((shares,)),
        ],
    )(recv, ids[None, :].astype(f32), owner, foot, movie)

    got = lax.all_to_all(send, "frame", 0, 0)

    kept, ratio = call(
        second_kernel,
        homes * tiles,
        out_shape=(
            jax.ShapeDtypeStruct((slot_total, width // shares), f32),
            jax.ShapeDtypeStruct((4 * tiles, frames), f32),
        ),
        in_specs=[pl.BlockSpec(memory_space=pltpu.SMEM), vmem, vmem, vmem, vmem, anywhere, anywhere],
        out_specs=(vmem, vmem),
        scratch_shapes=[
            pltpu.VMEM(movie.shape, bf16),
            pltpu.VMEM((slot_total, width), f32),
            pltpu.VMEM((4 * tiles, frames), f32),
            pltpu.VMEM((4 * tiles, frames), f32),
            pltpu.VMEM((16, lane), f32),
            pltpu.SemaphoreType.DMA((groups,)),
            pltpu.SemaphoreType.DMA((groups,)),
        ],
    )(frame[None].astype(jnp.int32), got, rows, owner, ids[:, None], foot, movie)

    back = lax.all_to_all(ratio.reshape(tiles, 4, frames), "tile", 0, 0)
    twice = jnp.concatenate([back, back], 0)
    home_rows = lax.dynamic_slice_in_dim(twice, tile, tiles, 0)[:, :per_pair]
    step = home_rows.transpose(1, 0, 2).reshape(homes, frames)
    traces_new = jnp.maximum(traces + step, 0.0)
    return kept.reshape(blocks, slots, width // shares), traces_new


def solution(mesh):
    return jax.shard_map(
        local,
        mesh=mesh,
        in_specs=(
            P("tile", "frame"),
            P("tile", None, None),
            P("tile", "frame"),
            P("tile", None),
            P("tile", None),
        ),
        out_specs=(P("tile", None, "frame"), P("tile", "frame")),
        check_vma=False,
    )
```

```python
import jax
import jax.numpy as jnp
from jax import lax
from jax.experimental import pallas as pl
from jax.experimental.pallas import tpu as pltpu
from jax.sharding import PartitionSpec as P

sparsity = 50.0
lane = 128
head = 32
ahead = 3
f32, bf16 = jnp.float32, jnp.bfloat16
nn = (((1,), (0,)), ((), ()))
nt = (((1,), (1,)), ((), ()))


def dot(a, b, dims=nn):
    return lax.dot_general(a, b, dims, preferred_element_type=f32)


def halves(x):
    high = x.astype(bf16)
    return high, (x - high.astype(f32)).astype(bf16)


def masks():
    row = lax.broadcasted_iota(jnp.int32, (lane, lane), 0)
    col = lax.broadcasted_iota(jnp.int32, (lane, lane), 1)
    return row == col, (row // 8) == (col // 8)


def column(eye, row):
    return jnp.sum(jnp.where(eye, row, 0.0), axis=1, keepdims=True)


def fetches(first, groups, voxels, movie_hbm, foot_hbm, movie, foot, sem_m, sem_f):
    def movie_copy(g):
        return pltpu.make_async_copy(
            movie_hbm.at[pl.ds((first + g) * voxels, voxels)], movie.at[pl.ds(g * voxels, voxels)], sem_m.at[g]
        )

    def foot_copy(g):
        return pltpu.make_async_copy(
            foot_hbm.at[pl.ds((first + g) * lane, lane)], foot.at[pl.ds(g * lane, lane)], sem_f.at[g]
        )

    def ready(g):
        movie_copy(g).wait()
        if g + ahead < groups:
            movie_copy(g + ahead).start()

    for g in range(groups):
        foot_copy(g).start()
    for g in range(min(ahead, groups)):
        movie_copy(g).start()
    return ready, foot_copy


def first_kernel(
    first, groups, recv, id_row, owner, foot_hbm, movie_hbm, rows, exact, packed, movie, foot, grams, mixed, sem_m, sem_f
):
    voxels = movie.shape[0] // groups
    ready, foot_copy = fetches(first, groups, voxels, movie_hbm, foot_hbm, movie, foot, sem_m, sem_f)

    eye, block = masks()
    names = id_row[...]
    sources = recv[...]
    for g in range(groups):
        own = column(eye, owner[g : g + 1, :].astype(f32))
        rows[g * lane : (g + 1) * lane, :] = dot((own == names).astype(bf16), sources).astype(bf16)
    diagonals = []
    for g in range(groups):
        at = slice(g * lane, (g + 1) * lane)
        gram = jnp.where(block, dot(rows[at, :], rows[at, :], nt), 0.0)
        diagonals.append(jnp.sum(jnp.where(eye, gram, 0.0), axis=0, keepdims=True))
        high, low = halves(gram)
        grams[at, :lane] = high
        grams[at, lane:] = low
    diagonal = jnp.concatenate(diagonals + [jnp.zeros((16 - groups, lane), f32)], 0)
    exact[0:16, :] = diagonal
    high, low = halves(diagonal)
    packed[0:16, :] = high
    packed[16:32, :] = low
    for g in range(groups):
        at = slice(g * lane, (g + 1) * lane)
        foot_copy(g).wait()
        high, low = halves(foot[at, :])
        mixed[at, :] = dot(grams[at, :], jnp.concatenate([high, high], 0)) + dot(grams[at, :lane], low)
    for g in range(groups):
        ready(g)
        for p in range(8):
            start = g * lane + p * 16
            both = dot(rows[start : start + 16, :], movie[g * voxels + p * 256 : g * voxels + (p + 1) * 256, :], nt)
            corr = jnp.concatenate([both[:8, :lane], both[8:, lane:]], 0)
            part = corr - mixed[start : start + 16, :]
            exact[16 + start : 32 + start, :] = part
            packed[head + start : head + start + 16, :] = part.astype(bf16)


def join_kernel(mine, got, exact, packed):
    diagonal = mine[0:16, :] + got[0:16, :].astype(f32) + got[16:32, :].astype(f32)
    exact[0:16, :] = diagonal
    high, low = halves(diagonal)
    packed[0:16, :] = high
    packed[16:32, :] = low
    rest = mine[16:, :] + got[head:, :].astype(f32)
    exact[16:, :] = rest
    packed[head:, :] = rest.astype(bf16)


def leaving_kernel(tile, traces, out, spread):
    tiles = out.shape[0] // 4
    for j in range(4):
        if j * tiles < traces.shape[0]:
            piece = pltpu.roll(traces[j * tiles : (j + 1) * tiles, :], tile[0], 0)
        else:
            piece = jnp.zeros((tiles, lane), f32)
        spread[pl.ds(j, tiles, stride=4), :] = piece
    out[...] = spread[...].astype(bf16)


def home_kernel(tile, back, traces, out):
    tiles = back.shape[0] // 4
    shift = lax.rem(tiles - tile[0], tiles)
    for j in range(traces.shape[0] // tiles):
        at = slice(j * tiles, (j + 1) * tiles)
        step = pltpu.roll(back[pl.ds(j, tiles, stride=4), :], shift, 0)
        out[at, :] = jnp.maximum(traces[at, :] + step, 0.0)


def second_kernel(first, groups, total_neurons, begin, end, *refs):
    quarter, owner, id_col, rows, foot_hbm, movie_hbm = refs[:6]
    rest = list(refs[6:])
    mine, got = rest.pop(0), rest.pop(0)
    before = None if begin else (rest.pop(0), rest.pop(0))
    kept = rest.pop(0)
    after = [rest.pop(0)] if end else [rest.pop(0), rest.pop(0)]
    movie, foot, updated, crosses, grads, sem_m, sem_f = rest
    voxels = movie.shape[0] // groups
    width = kept.shape[1]
    ready, foot_copy = fetches(first, groups, voxels, movie_hbm, foot_hbm, movie, foot, sem_m, sem_f)
    eye, block = masks()
    low_rows = lax.broadcasted_iota(jnp.int32, (16, lane), 0) < 8
    shift = lax.rem(lane - quarter[0] * width, lane)
    owners = owner[...]
    total = mine[0:16, :] + got[0:16, :].astype(f32) + got[16:32, :].astype(f32)
    inverse = jnp.where(owners < total_neurons, 1.0 / total[:groups], 0.0)
    for g in range(groups):
        at = slice(g * lane, (g + 1) * lane)
        scale = column(eye, inverse[g : g + 1, :])
        residual = mine[16 + g * lane : 16 + (g + 1) * lane, :]
        residual += got[head + g * lane : head + (g + 1) * lane, :].astype(f32)
        foot_copy(g).wait()
        new = jnp.maximum(foot[at, :] + (residual - sparsity) * scale, 0.0)
        new = jnp.where(scale > 0.0, new, 0.0)
        updated[at, :] = new
        kept[at, :] = pltpu.roll(new, shift, 1)[:, :width]
    norms = []
    for g in range(groups):
        at = slice(g * lane, (g + 1) * lane)
        high, low = halves(updated[at, :])
        cross = dot(jnp.concatenate([high, low], 1), jnp.concatenate([high, high], 1), nt) + dot(high, low, nt)
        cross = jnp.where(block, cross, 0.0)
        norms.append(jnp.sum(jnp.where(eye, cross, 0.0), axis=0, keepdims=True))
        high, low = halves(cross)
        crosses[at, :lane] = high
        crosses[at, lane:] = low
    for g in range(groups):
        at = slice(g * lane, (g + 1) * lane)
        ready(g)
        known = dot(crosses[at, :], jnp.concatenate([rows[at, :], rows[at, :]], 0))
        for p in range(8):
            two = slice(g * voxels + p * 256, g * voxels + (p + 1) * 256)
            part = updated[g * lane + 16 * p : g * lane + 16 * p + 16, :]
            wide = jnp.concatenate([jnp.where(low_rows, part, 0.0), jnp.where(low_rows, 0.0, part)], 1)
            grad = dot(wide.astype(bf16), movie[two, :]) - known[16 * p : 16 * p + 16]
            high, low = halves(grad)
            start = g * 2 * lane + 16 * p
            grads[start : start + 16, :] = high
            grads[start + lane : start + lane + 16, :] = low
    names = id_col[...]
    trace_grad = jnp.zeros(after[0].shape, f32) if begin else before[0][...]
    weight = jnp.zeros(after[0].shape, f32) if begin else before[1][...]
    for g in range(groups):
        picks = owners[g : g + 1, :] == names
        onehot = picks.astype(f32).astype(bf16)
        trace_grad += dot(jnp.concatenate([onehot, onehot], 1), grads[g * 2 * lane : (g + 1) * 2 * lane, :])
        weight += jnp.where(picks, norms[g], 0.0)
    if end:
        after[0][...] = trace_grad / jnp.maximum(jnp.sum(weight, axis=1, keepdims=True), 1.0)
    else:
        after[0][...] = trace_grad
        after[1][...] = weight


def local(movie, footprint, traces, slot_neuron, neuron_blocks):
    tiles, shares = lax.axis_size("tile"), lax.axis_size("frame")
    blocks, slots, width = footprint.shape
    homes, frames = traces.shape
    per_pair = homes // tiles
    slot_total = blocks * slots
    groups = slot_total // lane
    tile = lax.axis_index("tile")
    frame = lax.axis_index("frame")

    anywhere = pl.BlockSpec(memory_space=pl.ANY)
    vmem = pl.BlockSpec(memory_space=pltpu.VMEM)
    params = pltpu.CompilerParams(vmem_limit_bytes=32 * 1024 * 1024)

    def call(kernel, *static, **kw):
        return pl.pallas_call(lambda *refs: kernel(*static, *refs), compiler_params=params, **kw)

    def near(x):
        return pltpu.with_memory_space_constraint(x, pltpu.VMEM)

    def far(x):
        return pltpu.with_memory_space_constraint(x, pltpu.HBM)

    here = tile[None].astype(jnp.int32)
    smem = pl.BlockSpec(memory_space=pltpu.SMEM)
    leaving = call(
        leaving_kernel,
        out_shape=pltpu.HBM((4 * tiles, frames), bf16),
        in_specs=[smem, vmem],
        out_specs=vmem,
        scratch_shapes=[pltpu.VMEM((4 * tiles, frames), f32)],
    )(here, traces)
    recv = lax.all_to_all(leaving.reshape(tiles, 4, frames), "tile", 0, 0).reshape(4 * tiles, frames)

    k = jnp.arange(4 * tiles, dtype=jnp.int32)
    home, j = k // 4, k % 4
    ids = jnp.where(j < per_pair, homes * home + tiles * j + (tile + tiles - home) % tiles, -1)
    owner = slot_neuron.reshape(groups, lane)
    foot = footprint.reshape(slot_total, width)

    chunks = 2
    each = groups // chunks
    tall = each * lane + head
    id_row, id_col = near(ids[None, :].astype(f32)), near(ids[:, None])
    recv = near(recv)
    size = movie.shape[0] // chunks
    part_scratch = [pltpu.VMEM((size, frames), bf16), pltpu.VMEM((each * lane, width), f32)]
    fetch_sems = [pltpu.SemaphoreType.DMA((each,)), pltpu.SemaphoreType.DMA((each,))]
    owners = [near(owner[c * each : (c + 1) * each]) for c in range(chunks)]
    exact_shape, sent_shape = pltpu.VMEM((each * lane + 16, width), f32), pltpu.VMEM((tall, width), bf16)
    pairs = [[(s, s ^ 1) for s in range(shares)], [(s, shares - 1 - s) for s in range(shares)]]
    rows, mine, got = [], [], []
    for c in range(chunks):
        one, exact, sent = call(
            first_kernel,
            c * each,
            each,
            out_shape=(pltpu.VMEM((each * lane, frames), bf16), exact_shape, sent_shape),
            in_specs=[vmem, vmem, vmem, anywhere, anywhere],
            out_specs=(vmem,) * 3,
            scratch_shapes=part_scratch
            + [
                pltpu.VMEM((each * lane, 2 * lane), bf16),
                pltpu.VMEM((each * lane, width), f32),
            ]
            + fetch_sems,
        )(recv, id_row, owners[c], far(foot), far(movie))
        rows.append(one)
        mine.append(exact)
        got.append(lax.ppermute(sent, "frame", pairs[c % 2]))
    for c in range(chunks):
        mine[c], sent = call(
            join_kernel, out_shape=(exact_shape, sent_shape), in_specs=[vmem] * 2, out_specs=(vmem,) * 2
        )(near(mine[c]), near(got[c]))
        got[c] = lax.ppermute(sent, "frame", pairs[1 - c % 2])

    kept, running = [], []
    for c in range(chunks):
        begin, end = c == 0, c == chunks - 1
        total_shape = (4 * tiles, frames)
        outs = [jax.ShapeDtypeStruct((each * lane, width // shares), f32)]
        outs += [pltpu.HBM(total_shape, f32)] if end else [pltpu.VMEM(total_shape, f32)] * 2
        one, *running = call(
            second_kernel,
            c * each,
            each,
            homes * tiles,
            begin,
            end,
            out_shape=tuple(outs),
            in_specs=[smem]
            + [vmem] * 3
            + [anywhere] * 2
            + [vmem] * (2 + len(running)),
            out_specs=(vmem,) * len(outs),
            scratch_shapes=part_scratch
            + [
                pltpu.VMEM((each * lane, width), f32),
                pltpu.VMEM((each * lane, 2 * lane), bf16),
                pltpu.VMEM((2 * each * lane, frames), bf16),
            ]
            + fetch_sems,
        )(
            frame[None].astype(jnp.int32),
            owners[c],
            id_col,
            near(rows[c]),
            far(foot),
            far(movie),
            near(mine[c]),
            near(got[c]),
            *[near(x) for x in running],
        )
        kept.append(one)
    kept = jnp.concatenate(kept, 0) if chunks > 1 else kept[0]
    ratio = running[0]

    back = lax.all_to_all(ratio.reshape(tiles, 4, frames), "tile", 0, 0)
    traces_new = call(
        home_kernel,
        out_shape=jax.ShapeDtypeStruct(traces.shape, f32),
        in_specs=[smem, vmem, vmem],
        out_specs=vmem,
    )(here, near(back.reshape(4 * tiles, frames)), traces)
    return kept.reshape(blocks, slots, width // shares), traces_new


def solution(mesh):
    return jax.shard_map(
        local,
        mesh=mesh,
        in_specs=(
            P("tile", "frame"),
            P("tile", None, None),
            P("tile", "frame"),
            P("tile", None),
            P("tile", None),
        ),
        out_specs=(P("tile", None, "frame"), P("tile", "frame")),
        check_vma=False,
    )
```

```python
import jax
import jax.numpy as jnp
from jax import lax
from jax.experimental import pallas as pl
from jax.experimental.pallas import tpu as pltpu
from jax.sharding import PartitionSpec as P

sparsity = 50.0
lane = 128
head = 32
ahead = 3
f32, bf16 = jnp.float32, jnp.bfloat16
nn = (((1,), (0,)), ((), ()))
nt = (((1,), (1,)), ((), ()))


def dot(a, b, dims=nn):
    return lax.dot_general(a, b, dims, preferred_element_type=f32)


def halves(x):
    high = x.astype(bf16)
    return high, (x - high.astype(f32)).astype(bf16)


def masks():
    row = lax.broadcasted_iota(jnp.int32, (lane, lane), 0)
    col = lax.broadcasted_iota(jnp.int32, (lane, lane), 1)
    return row == col, (row // 8) == (col // 8)


def column(eye, row):
    return jnp.sum(jnp.where(eye, row, 0.0), axis=1, keepdims=True)


def residents(tile, homes, tiles, axis):
    shape = (1, 4 * tiles) if axis else (4 * tiles, 1)
    k = lax.broadcasted_iota(jnp.int32, shape, axis)
    home, j = lax.div(k, 4), lax.rem(k, 4)
    name = homes * home + tiles * j + lax.rem(tile + tiles - home, tiles)
    return jnp.where(j < homes // tiles, name, -1)


def fetches(first, groups, voxels, movie_hbm, foot_hbm, movie, foot, sem_m, sem_f):
    def movie_copy(g):
        return pltpu.make_async_copy(
            movie_hbm.at[pl.ds((first + g) * voxels, voxels)], movie.at[pl.ds(g * voxels, voxels)], sem_m.at[g]
        )

    def foot_copy(g):
        return pltpu.make_async_copy(
            foot_hbm.at[pl.ds((first + g) * lane, lane)], foot.at[pl.ds(g * lane, lane)], sem_f.at[g]
        )

    def ready(g):
        movie_copy(g).wait()
        if g + ahead < groups:
            movie_copy(g + ahead).start()

    for g in range(groups):
        foot_copy(g).start()
    for g in range(min(ahead, groups)):
        movie_copy(g).start()
    return ready, foot_copy


def first_kernel(
    first, groups, homes, tiles, place, recv, owner, foot_hbm, movie_hbm, rows, exact, packed, movie, foot, grams, mixed, sem_m, sem_f
):
    voxels = movie.shape[0] // groups
    ready, foot_copy = fetches(first, groups, voxels, movie_hbm, foot_hbm, movie, foot, sem_m, sem_f)

    eye, block = masks()
    names = residents(place[0], homes, tiles, 1).astype(f32)
    sources = recv[...]
    for g in range(groups):
        own = column(eye, owner[first + g : first + g + 1, :].astype(f32))
        rows[g * lane : (g + 1) * lane, :] = dot((own == names).astype(bf16), sources).astype(bf16)
    diagonals = []
    for g in range(groups):
        at = slice(g * lane, (g + 1) * lane)
        gram = jnp.where(block, dot(rows[at, :], rows[at, :], nt), 0.0)
        diagonals.append(jnp.sum(jnp.where(eye, gram, 0.0), axis=0, keepdims=True))
        high, low = halves(gram)
        grams[at, :lane] = high
        grams[at, lane:] = low
    diagonal = jnp.concatenate(diagonals + [jnp.zeros((16 - groups, lane), f32)], 0)
    exact[0:16, :] = diagonal
    high, low = halves(diagonal)
    packed[0:16, :] = high
    packed[16:32, :] = low
    for g in range(groups):
        at = slice(g * lane, (g + 1) * lane)
        foot_copy(g).wait()
        high, low = halves(foot[at, :])
        mixed[at, :] = dot(grams[at, :], jnp.concatenate([high, high], 0)) + dot(grams[at, :lane], low)
    for g in range(groups):
        ready(g)
        for p in range(8):
            start = g * lane + p * 16
            both = dot(rows[start : start + 16, :], movie[g * voxels + p * 256 : g * voxels + (p + 1) * 256, :], nt)
            corr = jnp.concatenate([both[:8, :lane], both[8:, lane:]], 0)
            part = corr - mixed[start : start + 16, :]
            exact[16 + start : 32 + start, :] = part
            packed[head + start : head + start + 16, :] = part.astype(bf16)


def join_kernel(mine, got, exact, packed):
    diagonal = mine[0:16, :] + got[0:16, :].astype(f32) + got[16:32, :].astype(f32)
    exact[0:16, :] = diagonal
    high, low = halves(diagonal)
    packed[0:16, :] = high
    packed[16:32, :] = low
    rest = mine[16:, :] + got[head:, :].astype(f32)
    exact[16:, :] = rest
    packed[head:, :] = rest.astype(bf16)


def leaving_kernel(tile, traces, out, spread):
    tiles = out.shape[0] // 4
    for j in range(4):
        if j * tiles < traces.shape[0]:
            piece = pltpu.roll(traces[j * tiles : (j + 1) * tiles, :], tile[0], 0)
        else:
            piece = jnp.zeros((tiles, lane), f32)
        spread[pl.ds(j, tiles, stride=4), :] = piece
    out[...] = spread[...].astype(bf16)


def home_kernel(tile, back, traces, out):
    tiles = back.shape[0] // 4
    shift = lax.rem(tiles - tile[0], tiles)
    for j in range(traces.shape[0] // tiles):
        at = slice(j * tiles, (j + 1) * tiles)
        step = pltpu.roll(back[pl.ds(j, tiles, stride=4), :], shift, 0)
        out[at, :] = jnp.maximum(traces[at, :] + step, 0.0)


def second_kernel(first, groups, homes, tiles, begin, end, *refs):
    place, owner, rows, foot, movie, mine, got = refs[:7]
    rest = list(refs[7:])
    before = None if begin else (rest.pop(0), rest.pop(0))
    if not begin:
        rest.pop(0)
    kept = rest.pop(0)
    after = [rest.pop(0)] if end else [rest.pop(0), rest.pop(0)]
    updated, crosses, grads = rest
    voxels = movie.shape[0] // groups
    width = kept.shape[1]
    eye, block = masks()
    low_rows = lax.broadcasted_iota(jnp.int32, (16, lane), 0) < 8
    shift = lax.rem(lane - place[1] * width, lane)
    owners = owner[first : first + groups, :]
    total = mine[0:16, :] + got[0:16, :].astype(f32) + got[16:32, :].astype(f32)
    inverse = jnp.where(owners < homes * tiles, 1.0 / total[:groups], 0.0)
    for g in range(groups):
        at = slice(g * lane, (g + 1) * lane)
        scale = column(eye, inverse[g : g + 1, :])
        residual = mine[16 + g * lane : 16 + (g + 1) * lane, :]
        residual += got[head + g * lane : head + (g + 1) * lane, :].astype(f32)
        new = jnp.maximum(foot[at, :] + (residual - sparsity) * scale, 0.0)
        new = jnp.where(scale > 0.0, new, 0.0)
        updated[at, :] = new
        kept[(first + g) * lane : (first + g + 1) * lane, :] = pltpu.roll(new, shift, 1)[:, :width]
    norms = []
    for g in range(groups):
        at = slice(g * lane, (g + 1) * lane)
        high, low = halves(updated[at, :])
        cross = dot(jnp.concatenate([high, low], 1), jnp.concatenate([high, high], 1), nt) + dot(high, low, nt)
        cross = jnp.where(block, cross, 0.0)
        norms.append(jnp.sum(jnp.where(eye, cross, 0.0), axis=0, keepdims=True))
        high, low = halves(cross)
        crosses[at, :lane] = high
        crosses[at, lane:] = low
    for g in range(groups):
        at = slice(g * lane, (g + 1) * lane)
        known = dot(crosses[at, :], jnp.concatenate([rows[at, :], rows[at, :]], 0))
        for p in range(8):
            two = slice(g * voxels + p * 256, g * voxels + (p + 1) * 256)
            part = updated[g * lane + 16 * p : g * lane + 16 * p + 16, :]
            wide = jnp.concatenate([jnp.where(low_rows, part, 0.0), jnp.where(low_rows, 0.0, part)], 1)
            grad = dot(wide.astype(bf16), movie[two, :]) - known[16 * p : 16 * p + 16]
            high, low = halves(grad)
            start = g * 2 * lane + 16 * p
            grads[start : start + 16, :] = high
            grads[start + lane : start + lane + 16, :] = low
    names = residents(place[0], homes, tiles, 0)
    trace_grad = jnp.zeros(after[0].shape, f32) if begin else before[0][...]
    weight = jnp.zeros(after[0].shape, f32) if begin else before[1][...]
    for g in range(groups):
        picks = owners[g : g + 1, :] == names
        onehot = picks.astype(f32).astype(bf16)
        trace_grad += dot(jnp.concatenate([onehot, onehot], 1), grads[g * 2 * lane : (g + 1) * 2 * lane, :])
        weight += jnp.where(picks, norms[g], 0.0)
    if end:
        after[0][...] = trace_grad / jnp.maximum(jnp.sum(weight, axis=1, keepdims=True), 1.0)
    else:
        after[0][...] = trace_grad
        after[1][...] = weight


def local(movie, footprint, traces, slot_neuron, neuron_blocks):
    tiles, shares = lax.axis_size("tile"), lax.axis_size("frame")
    blocks, slots, width = footprint.shape
    homes, frames = traces.shape
    per_pair = homes // tiles
    slot_total = blocks * slots
    groups = slot_total // lane
    tile = lax.axis_index("tile")
    frame = lax.axis_index("frame")

    anywhere = pl.BlockSpec(memory_space=pl.ANY)
    vmem = pl.BlockSpec(memory_space=pltpu.VMEM)
    params = pltpu.CompilerParams(vmem_limit_bytes=32 * 1024 * 1024)

    def call(kernel, *static, **kw):
        return pl.pallas_call(lambda *refs: kernel(*static, *refs), compiler_params=params, **kw)

    def near(x):
        return pltpu.with_memory_space_constraint(x, pltpu.VMEM)

    def far(x):
        return pltpu.with_memory_space_constraint(x, pltpu.HBM)

    here = jnp.stack([tile, frame]).astype(jnp.int32)
    smem = pl.BlockSpec(memory_space=pltpu.SMEM)
    leaving = call(
        leaving_kernel,
        out_shape=pltpu.HBM((4 * tiles, frames), bf16),
        in_specs=[smem, vmem],
        out_specs=vmem,
        scratch_shapes=[pltpu.VMEM((4 * tiles, frames), f32)],
    )(here, far(traces))
    recv = lax.all_to_all(leaving.reshape(tiles, 4, frames), "tile", 0, 0).reshape(4 * tiles, frames)

    owner = slot_neuron.reshape(groups, lane)
    foot = footprint.reshape(slot_total, width)

    chunks = 2
    each = groups // chunks
    tall = each * lane + head
    recv = near(recv)
    size = movie.shape[0] // chunks
    owner = near(owner)
    exact_shape, sent_shape = pltpu.VMEM((each * lane + 16, width), f32), pltpu.VMEM((tall, width), bf16)
    pairs = [[(s, s ^ 1) for s in range(shares)], [(s, shares - 1 - s) for s in range(shares)]]
    held, mine, got = [], [], []
    for c in range(chunks):
        row, exact, sent, film, shapes = call(
            first_kernel,
            c * each,
            each,
            homes,
            tiles,
            out_shape=(
                pltpu.VMEM((each * lane, frames), bf16),
                exact_shape,
                sent_shape,
                pltpu.VMEM((size, frames), bf16),
                pltpu.VMEM((each * lane, width), f32),
            ),
            in_specs=[smem, vmem, vmem, anywhere, anywhere],
            out_specs=(vmem,) * 5,
            scratch_shapes=[
                pltpu.VMEM((each * lane, 2 * lane), bf16),
                pltpu.VMEM((each * lane, width), f32),
                pltpu.SemaphoreType.DMA((each,)),
                pltpu.SemaphoreType.DMA((each,)),
            ],
        )(here, recv, owner, far(foot), far(movie))
        held.append((near(row), near(shapes), near(film)))
        mine.append(exact)
        got.append(lax.ppermute(sent, "frame", pairs[c % 2]))
    for c in range(chunks):
        mine[c], sent = call(
            join_kernel, out_shape=(exact_shape, sent_shape), in_specs=[vmem] * 2, out_specs=(vmem,) * 2
        )(near(mine[c]), near(got[c]))
        got[c] = lax.ppermute(sent, "frame", pairs[1 - c % 2])

    kept, running = None, []
    for c in range(chunks):
        begin, end = c == 0, c == chunks - 1
        total_shape = (4 * tiles, frames)
        outs = [pltpu.VMEM((slot_total, width // shares), f32)]
        outs += [pltpu.HBM(total_shape, f32)] if end else [pltpu.VMEM(total_shape, f32)] * 2
        old = [] if begin else [near(x) for x in running + [kept]]
        kept, *running = call(
            second_kernel,
            c * each,
            each,
            homes,
            tiles,
            begin,
            end,
            out_shape=tuple(outs),
            in_specs=[smem] + [vmem] * (6 + len(old)),
            out_specs=(vmem,) * len(outs),
            scratch_shapes=[
                pltpu.VMEM((each * lane, width), f32),
                pltpu.VMEM((each * lane, 2 * lane), bf16),
                pltpu.VMEM((2 * each * lane, frames), bf16),
            ],
            input_output_aliases={} if begin else {9: 0},
        )(here, owner, *held[c], near(mine[c]), near(got[c]), *old)
    ratio = running[0]

    back = lax.all_to_all(ratio.reshape(tiles, 4, frames), "tile", 0, 0)
    traces_new = call(
        home_kernel,
        out_shape=jax.ShapeDtypeStruct(traces.shape, f32),
        in_specs=[smem, vmem, vmem],
        out_specs=vmem,
    )(here, near(back.reshape(4 * tiles, frames)), traces)
    return kept.reshape(blocks, slots, width // shares), traces_new


def solution(mesh):
    return jax.shard_map(
        local,
        mesh=mesh,
        in_specs=(
            P("tile", "frame"),
            P("tile", None, None),
            P("tile", "frame"),
            P("tile", None),
            P("tile", None),
        ),
        out_specs=(P("tile", None, "frame"), P("tile", "frame")),
        check_vma=False,
    )
```

```python
import jax
import jax.numpy as jnp
from jax import lax
from jax.experimental import pallas as pl
from jax.experimental.pallas import tpu as pltpu
from jax.sharding import PartitionSpec as P

sparsity = 50.0
lane = 128
head = 32
f32, bf16 = jnp.float32, jnp.bfloat16
nn = (((1,), (0,)), ((), ()))
nt = (((1,), (1,)), ((), ()))


def dot(a, b, dims=nn):
    return lax.dot_general(a, b, dims, preferred_element_type=f32)


def halves(x):
    high = x.astype(bf16)
    return high, (x - high.astype(f32)).astype(bf16)


def masks():
    row = lax.broadcasted_iota(jnp.int32, (lane, lane), 0)
    col = lax.broadcasted_iota(jnp.int32, (lane, lane), 1)
    return row == col, (row // 8) == (col // 8)


def column(eye, row):
    return jnp.sum(jnp.where(eye, row, 0.0), axis=1, keepdims=True)


def residents(tile, homes, tiles, axis):
    shape = (1, 4 * tiles) if axis else (4 * tiles, 1)
    k = lax.broadcasted_iota(jnp.int32, shape, axis)
    home, j = lax.div(k, 4), lax.rem(k, 4)
    name = homes * home + tiles * j + lax.rem(tile + tiles - home, tiles)
    return jnp.where(j < homes // tiles, name, -1)


def load_kernel(movie_hbm, movie, sem):
    copy = pltpu.make_async_copy(movie_hbm.at[pl.ds(0, movie.shape[0])], movie, sem)
    copy.start()
    copy.wait()


def first_kernel(first, groups, held, voxels, homes, tiles, *refs):
    place, recv, owner, movie, foot_hbm, movie_hbm, rows, exact, packed, foot, piece, grams, sem_f, sem_m = refs
    foot_copy = pltpu.make_async_copy(foot_hbm.at[pl.ds(first * lane, groups * lane)], foot, sem_f)
    piece_copy = pltpu.make_async_copy(
        movie_hbm.at[pl.ds((first + held) * voxels, piece.shape[0])], piece, sem_m
    )
    foot_copy.start()
    piece_copy.start()
    eye, block = masks()
    names = residents(place[0], homes, tiles, 1).astype(f32)
    sources = recv[...]
    for g in range(groups):
        own = column(eye, owner[first + g : first + g + 1, :].astype(f32))
        rows[g * lane : (g + 1) * lane, :] = dot((own == names).astype(bf16), sources).astype(bf16)
    for g in range(groups):
        if g == held:
            piece_copy.wait()
        film, where = (movie, g * voxels) if g < held else (piece, (g - held) * voxels)
        for p in range(8):
            start = g * lane + p * 16
            both = dot(rows[start : start + 16, :], film[where + p * 256 : where + (p + 1) * 256, :], nt)
            exact[16 + start : 32 + start, :] = jnp.concatenate([both[:8, :lane], both[8:, lane:]], 0)
    diagonals = []
    for g in range(groups):
        at = slice(g * lane, (g + 1) * lane)
        gram = jnp.where(block, dot(rows[at, :], rows[at, :], nt), 0.0)
        diagonals.append(jnp.sum(jnp.where(eye, gram, 0.0), axis=0, keepdims=True))
        high, low = halves(gram)
        grams[at, :lane] = high
        grams[at, lane:] = low
    diagonal = jnp.concatenate(diagonals + [jnp.zeros((16 - groups, lane), f32)], 0)
    exact[0:16, :] = diagonal
    high, low = halves(diagonal)
    packed[0:16, :] = high
    packed[16:32, :] = low
    foot_copy.wait()
    for g in range(groups):
        at = slice(g * lane, (g + 1) * lane)
        high, low = halves(foot[at, :])
        mixed = dot(grams[at, :], jnp.concatenate([high, high], 0)) + dot(grams[at, :lane], low)
        here = slice(16 + g * lane, 16 + (g + 1) * lane)
        part = exact[here, :] - mixed
        exact[here, :] = part
        packed[head + g * lane : head + (g + 1) * lane, :] = part.astype(bf16)
    if held == groups:
        piece_copy.wait()


def join_kernel(mine, got, exact, packed):
    diagonal = mine[0:16, :] + got[0:16, :].astype(f32) + got[16:32, :].astype(f32)
    exact[0:16, :] = diagonal
    high, low = halves(diagonal)
    packed[0:16, :] = high
    packed[16:32, :] = low
    rest = mine[16:, :] + got[head:, :].astype(f32)
    exact[16:, :] = rest
    packed[head:, :] = rest.astype(bf16)


def leaving_kernel(tile, traces, out, spread):
    tiles = out.shape[0] // 4
    for j in range(4):
        if j * tiles < traces.shape[0]:
            piece = pltpu.roll(traces[j * tiles : (j + 1) * tiles, :], tile[0], 0)
        else:
            piece = jnp.zeros((tiles, lane), f32)
        spread[pl.ds(j, tiles, stride=4), :] = piece
    out[...] = spread[...].astype(bf16)


def home_kernel(tile, back, traces, out, spread):
    tiles = back.shape[0] // 4
    spread[...] = back[...].astype(jnp.int32).astype(f32)
    unit = jnp.exp2(spread[pl.ds(3, tiles, stride=4), :])
    shift = lax.rem(tiles - tile[0], tiles)
    for j in range(traces.shape[0] // tiles):
        at = slice(j * tiles, (j + 1) * tiles)
        step = pltpu.roll(spread[pl.ds(j, tiles, stride=4), :] * unit, shift, 0)
        out[at, :] = jnp.maximum(traces[at, :] + step, 0.0)


def turn(updated, frame, turned):
    slots, width, _ = turned.shape
    blocks = updated.shape[0] // slots
    at_once = lane // width
    part = lax.broadcasted_iota(jnp.int32, (blocks, lane), 1) // width
    for first in range(0, slots, at_once):
        packed = jnp.zeros((blocks, lane), f32)
        for i in range(at_once):
            rows = updated[pl.ds(first + i, blocks, stride=slots), :]
            rows = pltpu.roll(rows, lax.rem(lane + (i - frame) * width, lane), 1)
            packed = jnp.where(part == i, rows, packed)
        packed = jnp.concatenate([packed, jnp.zeros((lane - blocks, lane), f32)], 0)
        turned[first : first + at_once, :, :] = packed.T.reshape(at_once, width, lane)


def join_turned(before, second, whole, blocks):
    after = pltpu.roll(second[...].reshape(-1, lane), blocks, 1)
    low = lax.broadcasted_iota(jnp.int32, after.shape, 1) < blocks
    both = jnp.where(low, before[...].reshape(-1, lane), after)
    whole[:, :, :lane] = both.reshape(before.shape)
    whole[:, :, lane:] = after.reshape(before.shape)[:, :, : whole.shape[2] - lane]


def second_kernel(first, groups, held, voxels, homes, tiles, begin, end, *refs):
    rest = list(refs)
    place, owner, rows, foot, movie, mine, got = [rest.pop(0) for _ in range(7)]
    piece = rest.pop(0) if held < groups else None
    before = None if begin else (rest.pop(0), rest.pop(0))
    turned_before = None if begin else rest.pop(0)
    turned = rest.pop(0)
    after = [rest.pop(0)] if end else [rest.pop(0), rest.pop(0)]
    updated, crosses, grads = rest[:3]
    eye, block = masks()
    low_rows = lax.broadcasted_iota(jnp.int32, (16, lane), 0) < 8
    owners = owner[first : first + groups, :]
    total = mine[0:16, :] + got[0:16, :].astype(f32) + got[16:32, :].astype(f32)
    inverse = jnp.where(owners < homes * tiles, 1.0 / total[:groups], 0.0)
    for g in range(groups):
        at = slice(g * lane, (g + 1) * lane)
        scale = column(eye, inverse[g : g + 1, :])
        residual = mine[16 + g * lane : 16 + (g + 1) * lane, :]
        residual += got[head + g * lane : head + (g + 1) * lane, :].astype(f32)
        new = jnp.maximum(foot[at, :] + (residual - sparsity) * scale, 0.0)
        new = jnp.where(scale > 0.0, new, 0.0)
        updated[at, :] = new
    if begin:
        turn(updated, place[1], turned)
    else:
        second, whole, sem_k = rest[3:]
        turn(updated, place[1], second)
        join_turned(turned_before, second, whole, first * lane // turned.shape[0])
        turned_copy = pltpu.make_async_copy(whole, turned, sem_k)
        turned_copy.start()
    norms = []
    for g in range(groups):
        at = slice(g * lane, (g + 1) * lane)
        high, low = halves(updated[at, :])
        cross = dot(jnp.concatenate([high, low], 1), jnp.concatenate([high, high], 1), nt) + dot(high, low, nt)
        cross = jnp.where(block, cross, 0.0)
        norms.append(jnp.sum(jnp.where(eye, cross, 0.0), axis=0, keepdims=True))
        high, low = halves(cross)
        crosses[at, :lane] = high
        crosses[at, lane:] = low
    for g in range(groups):
        at = slice(g * lane, (g + 1) * lane)
        known = dot(crosses[at, :], jnp.concatenate([rows[at, :], rows[at, :]], 0))
        film, where = (movie, g * voxels) if g < held else (piece, (g - held) * voxels)
        for p in range(8):
            two = slice(where + p * 256, where + (p + 1) * 256)
            part = updated[g * lane + 16 * p : g * lane + 16 * p + 16, :]
            wide = jnp.concatenate([jnp.where(low_rows, part, 0.0), jnp.where(low_rows, 0.0, part)], 1)
            grad = dot(wide.astype(bf16), film[two, :]) - known[16 * p : 16 * p + 16]
            high, low = halves(grad)
            start = g * 2 * lane + 16 * p
            grads[start : start + 16, :] = high
            grads[start + lane : start + lane + 16, :] = low
    names = residents(place[0], homes, tiles, 0)
    trace_grad = jnp.zeros(after[0].shape, f32) if begin else before[0][...]
    weight = jnp.zeros(after[0].shape, f32) if begin else before[1][...]
    for g in range(groups):
        picks = owners[g : g + 1, :] == names
        onehot = picks.astype(f32).astype(bf16)
        trace_grad += dot(jnp.concatenate([onehot, onehot], 1), grads[g * 2 * lane : (g + 1) * 2 * lane, :])
        weight += jnp.where(picks, norms[g], 0.0)
    if end:
        step = trace_grad / jnp.maximum(jnp.sum(weight, axis=1, keepdims=True), 1.0)
        largest = jnp.maximum(jnp.max(jnp.abs(step), axis=(0, 1), keepdims=True), 1e-30)
        power = jnp.ceil(jnp.log2(largest * (1.0 / 32700.0)))
        whole = jnp.round(step * jnp.exp2(-power))
        spare = lax.rem(lax.broadcasted_iota(jnp.int32, step.shape, 0), 4) == 3
        after[0][...] = jnp.where(spare, power, whole).astype(jnp.int32).astype(jnp.int16)
    else:
        after[0][...] = trace_grad
        after[1][...] = weight
    if not begin:
        turned_copy.wait()


def local(movie, footprint, traces, slot_neuron, neuron_blocks):
    tiles, shares = lax.axis_size("tile"), lax.axis_size("frame")
    blocks, slots, width = footprint.shape
    homes, frames = traces.shape
    per_pair = homes // tiles
    slot_total = blocks * slots
    groups = slot_total // lane
    tile = lax.axis_index("tile")
    frame = lax.axis_index("frame")

    anywhere = pl.BlockSpec(memory_space=pl.ANY)
    vmem = pl.BlockSpec(memory_space=pltpu.VMEM)
    params = pltpu.CompilerParams(vmem_limit_bytes=32 * 1024 * 1024)

    def call(kernel, *static, **kw):
        return pl.pallas_call(lambda *refs: kernel(*static, *refs), compiler_params=params, **kw)

    def near(x):
        return pltpu.with_memory_space_constraint(x, pltpu.VMEM)

    def far(x):
        return pltpu.with_memory_space_constraint(x, pltpu.HBM)

    here = jnp.stack([tile, frame]).astype(jnp.int32)
    smem = pl.BlockSpec(memory_space=pltpu.SMEM)
    leaving = call(
        leaving_kernel,
        out_shape=pltpu.HBM((4 * tiles, frames), bf16),
        in_specs=[smem, vmem],
        out_specs=vmem,
        scratch_shapes=[pltpu.VMEM((4 * tiles, frames), f32)],
    )(here, far(traces))
    recv = lax.all_to_all(leaving.reshape(tiles, 4, frames), "tile", 0, 0).reshape(4 * tiles, frames)

    owner = slot_neuron.reshape(groups, lane)
    foot = footprint.reshape(slot_total, width)

    voxels = movie.shape[0] // groups
    counts = [groups // 2, groups - groups // 2]
    firsts = [0, counts[0]]
    pieces = [counts[0], counts[1] - 1, 1]
    owner = near(owner)
    pairs = [[(s, s ^ 1) for s in range(shares)], [(s, shares - 1 - s) for s in range(shares)]]

    def exact_shape(c):
        return pltpu.VMEM((counts[c] * lane + 16, width), f32)

    def sent_shape(c):
        return pltpu.VMEM((counts[c] * lane + head, width), bf16)

    def film_shape(k):
        return pltpu.VMEM((pieces[k] * voxels, frames), bf16)

    film = call(
        load_kernel,
        out_shape=film_shape(0),
        in_specs=[anywhere],
        out_specs=vmem,
        scratch_shapes=[pltpu.SemaphoreType.DMA],
        cost_estimate=pl.CostEstimate(flops=0, bytes_accessed=2 * movie.size, transcendentals=0),
    )(far(movie))

    films, held, mine, got = [film], [], [], []
    for c in range(2):
        row, exact, sent, shapes, film = call(
            first_kernel,
            firsts[c],
            counts[c],
            pieces[c],
            voxels,
            homes,
            tiles,
            out_shape=(
                pltpu.VMEM((counts[c] * lane, frames), bf16),
                exact_shape(c),
                sent_shape(c),
                pltpu.VMEM((counts[c] * lane, width), f32),
                film_shape(c + 1),
            ),
            in_specs=[smem, vmem, vmem, vmem, anywhere, anywhere],
            out_specs=(vmem,) * 5,
            scratch_shapes=[pltpu.VMEM((counts[c] * lane, 2 * lane), bf16)] + [pltpu.SemaphoreType.DMA] * 2,
        )(here, recv, owner, near(films[c]), far(foot), far(movie))
        films.append(film)
        held.append([row, shapes])
        mine.append(exact)
        got.append(lax.ppermute(sent, "frame", pairs[c]))
    for c in range(2):
        mine[c], sent = call(
            join_kernel, out_shape=(exact_shape(c), sent_shape(c)), in_specs=[vmem] * 2, out_specs=(vmem,) * 2
        )(near(mine[c]), near(got[c]))
        got[c] = lax.ppermute(sent, "frame", pairs[1 - c])

    kept, running = None, []
    for c in range(2):
        begin, end = c == 0, c == 1
        total_shape = (4 * tiles, frames)
        outs = [pltpu.VMEM((slots, width // shares, lane), f32)] if begin else [pltpu.HBM((slots, width // shares, blocks), f32)]
        outs += [pltpu.VMEM(total_shape, jnp.int16)] if end else [pltpu.VMEM(total_shape, f32)] * 2
        more = [] if begin else [
            pltpu.VMEM((slots, width // shares, lane), f32),
            pltpu.VMEM((slots, width // shares, blocks), f32),
            pltpu.SemaphoreType.DMA,
        ]
        old = [] if begin else [films[2]] + running + [kept]
        given = [*held[c], films[c], mine[c], got[c], *old]
        kept, *running = call(
            second_kernel,
            firsts[c],
            counts[c],
            pieces[c],
            voxels,
            homes,
            tiles,
            begin,
            end,
            out_shape=tuple(outs),
            in_specs=[smem] + [vmem] * (1 + len(given)),
            out_specs=(vmem if begin else anywhere,) + (vmem,) * (len(outs) - 1),
            scratch_shapes=[
                pltpu.VMEM((counts[c] * lane, width), f32),
                pltpu.VMEM((counts[c] * lane, 2 * lane), bf16),
                pltpu.VMEM((2 * counts[c] * lane, frames), bf16),
            ]
            + more,
        )(here, owner, *[near(x) for x in given])
    ratio = running[0]

    back = lax.all_to_all(ratio.reshape(tiles, 4, frames), "tile", 0, 0)
    traces_new = call(
        home_kernel,
        out_shape=jax.ShapeDtypeStruct(traces.shape, f32),
        in_specs=[smem, vmem, vmem],
        out_specs=vmem,
        scratch_shapes=[pltpu.VMEM((4 * tiles, frames), f32)],
    )(here, near(back.reshape(4 * tiles, frames)), near(traces))
    return kept.transpose(2, 0, 1), traces_new


def solution(mesh):
    return jax.shard_map(
        local,
        mesh=mesh,
        in_specs=(
            P("tile", "frame"),
            P("tile", None, None),
            P("tile", "frame"),
            P("tile", None),
            P("tile", None),
        ),
        out_specs=(P("tile", None, "frame"), P("tile", "frame")),
        check_vma=False,
    )
```

```python
import jax
import jax.numpy as jnp
from jax import lax
from jax.experimental import pallas as pl
from jax.experimental.pallas import tpu as pltpu
from jax.sharding import PartitionSpec as P

sparsity = 50.0
lane = 128
head = 32
f32, bf16 = jnp.float32, jnp.bfloat16
nn = (((1,), (0,)), ((), ()))
nt = (((1,), (1,)), ((), ()))


def dot(a, b, dims=nn):
    return lax.dot_general(a, b, dims, preferred_element_type=f32)


def halves(x):
    high = x.astype(bf16)
    return high, (x - high.astype(f32)).astype(bf16)


def masks():
    row = lax.broadcasted_iota(jnp.int32, (lane, lane), 0)
    col = lax.broadcasted_iota(jnp.int32, (lane, lane), 1)
    return row == col, (row // 8) == (col // 8)


def column(eye, row):
    return jnp.sum(jnp.where(eye, row, 0.0), axis=1, keepdims=True)


def residents(tile, homes, tiles, axis):
    shape = (1, 4 * tiles) if axis else (4 * tiles, 1)
    k = lax.broadcasted_iota(jnp.int32, shape, axis)
    home, j = lax.div(k, 4), lax.rem(k, 4)
    name = homes * home + tiles * j + lax.rem(tile + tiles - home, tiles)
    return jnp.where(j < homes // tiles, name, -1)


def load_kernel(by_slot_hbm, movie_hbm, movie, owner, by_slot, sem, sem_s):
    slot_copy = pltpu.make_async_copy(by_slot_hbm, by_slot, sem_s)
    copy = pltpu.make_async_copy(movie_hbm.at[pl.ds(0, movie.shape[0])], movie, sem)
    slot_copy.start()
    copy.start()
    slots, blocks = by_slot.shape
    block = lax.broadcasted_iota(jnp.int32, (blocks, lane), 0)
    place = lax.broadcasted_iota(jnp.int32, (blocks, lane), 1)
    mine = lax.broadcasted_iota(jnp.int32, (slots, lane), 1) % slots
    mine = mine == lax.broadcasted_iota(jnp.int32, (slots, lane), 0)
    slot_copy.wait()
    names = by_slot[...]
    high = (names // 128).astype(f32).astype(bf16)
    low = (names % 128).astype(f32).astype(bf16)
    both = jnp.concatenate([high, low], 0)
    for g in range(owner.shape[0]):
        pick = (block == g * (lane // slots) + place // slots).astype(f32).astype(bf16)
        wide = dot(both, pick)
        wide = wide[:slots] * 128.0 + wide[slots:]
        row = jnp.sum(jnp.where(mine, wide, 0.0), axis=0, keepdims=True)
        owner[g : g + 1, :] = row.astype(jnp.int32)
    copy.wait()


def first_kernel(first, groups, held, voxels, homes, tiles, *refs):
    recv, owner, movie, foot_hbm, movie_hbm, rows, exact, packed, foot, piece, grams, sem_f, sem_m = refs
    foot_copy = pltpu.make_async_copy(foot_hbm.at[pl.ds(first * lane, groups * lane)], foot, sem_f)
    piece_copy = pltpu.make_async_copy(
        movie_hbm.at[pl.ds((first + held) * voxels, piece.shape[0])], piece, sem_m
    )
    for copy in (foot_copy, piece_copy) if held == groups else (piece_copy, foot_copy):
        copy.start()
    eye, block = masks()
    names = residents(lax.axis_index("tile"), homes, tiles, 1).astype(f32)
    sources = recv[...]
    for g in range(groups):
        own = column(eye, owner[first + g : first + g + 1, :].astype(f32))
        rows[g * lane : (g + 1) * lane, :] = dot((own == names).astype(bf16), sources).astype(bf16)
    for g in range(groups):
        if g == held:
            piece_copy.wait()
        film, where = (movie, g * voxels) if g < held else (piece, (g - held) * voxels)
        for p in range(8):
            start = g * lane + p * 16
            both = dot(rows[start : start + 16, :], film[where + p * 256 : where + (p + 1) * 256, :], nt)
            exact[16 + start : 32 + start, :] = jnp.concatenate([both[:8, :lane], both[8:, lane:]], 0)
    diagonals = []
    for g in range(groups):
        at = slice(g * lane, (g + 1) * lane)
        gram = jnp.where(block, dot(rows[at, :], rows[at, :], nt), 0.0)
        diagonals.append(jnp.sum(jnp.where(eye, gram, 0.0), axis=0, keepdims=True))
        high, low = halves(gram)
        grams[at, :lane] = high
        grams[at, lane:] = low
    diagonal = jnp.concatenate(diagonals + [jnp.zeros((16 - groups, lane), f32)], 0)
    exact[0:16, :] = diagonal
    high, low = halves(diagonal)
    packed[0:16, :] = high
    packed[16:32, :] = low
    foot_copy.wait()
    for g in range(groups):
        at = slice(g * lane, (g + 1) * lane)
        high, low = halves(foot[at, :])
        mixed = dot(grams[at, :], jnp.concatenate([high, high], 0)) + dot(grams[at, :lane], low)
        here = slice(16 + g * lane, 16 + (g + 1) * lane)
        part = exact[here, :] - mixed
        exact[here, :] = part
        packed[head + g * lane : head + (g + 1) * lane, :] = part.astype(bf16)
    if held == groups:
        piece_copy.wait()


def join_kernel(mine, got, exact, packed):
    diagonal = mine[0:16, :] + got[0:16, :].astype(f32) + got[16:32, :].astype(f32)
    exact[0:16, :] = diagonal
    high, low = halves(diagonal)
    packed[0:16, :] = high
    packed[16:32, :] = low
    rest = mine[16:, :] + got[head:, :].astype(f32)
    exact[16:, :] = rest
    packed[head:, :] = rest.astype(bf16)


def leaving_kernel(traces, out, spread):
    tiles = out.shape[0] // 4
    for j in range(4):
        if j * tiles < traces.shape[0]:
            piece = pltpu.roll(traces[j * tiles : (j + 1) * tiles, :], lax.axis_index("tile"), 0)
        else:
            piece = jnp.zeros((tiles, lane), f32)
        spread[pl.ds(j, tiles, stride=4), :] = piece
    out[...] = spread[...].astype(bf16)


def home_kernel(back, traces, turned, out_hbm, turned_hbm, spread, out, sem_t, sem_o):
    turned_copy = pltpu.make_async_copy(turned, turned_hbm, sem_t)
    turned_copy.start()
    tiles = back.shape[0] // 4
    spread[...] = back[...].astype(jnp.int32).astype(f32)
    unit = jnp.exp2(spread[pl.ds(3, tiles, stride=4), :])
    shift = lax.rem(tiles - lax.axis_index("tile"), tiles)
    for j in range(traces.shape[0] // tiles):
        at = slice(j * tiles, (j + 1) * tiles)
        step = pltpu.roll(spread[pl.ds(j, tiles, stride=4), :] * unit, shift, 0)
        out[at, :] = jnp.maximum(traces[at, :] + step, 0.0)
    out_copy = pltpu.make_async_copy(out, out_hbm, sem_o)
    out_copy.start()
    turned_copy.wait()
    out_copy.wait()


def turn(updated, frame, turned):
    slots, width, _ = turned.shape
    blocks = updated.shape[0] // slots
    at_once = lane // width
    part = lax.broadcasted_iota(jnp.int32, (blocks, lane), 1) // width
    for first in range(0, slots, at_once):
        packed = jnp.zeros((blocks, lane), f32)
        for i in range(at_once):
            rows = updated[pl.ds(first + i, blocks, stride=slots), :]
            rows = pltpu.roll(rows, lax.rem(lane + (i - frame) * width, lane), 1)
            packed = jnp.where(part == i, rows, packed)
        packed = jnp.concatenate([packed, jnp.zeros((lane - blocks, lane), f32)], 0)
        turned[first : first + at_once, :, :] = packed.T.reshape(at_once, width, lane)


def join_turned(before, second, whole, blocks):
    after = pltpu.roll(second[...].reshape(-1, lane), blocks, 1)
    low = lax.broadcasted_iota(jnp.int32, after.shape, 1) < blocks
    both = jnp.where(low, before[...].reshape(-1, lane), after)
    whole[:, :, :lane] = both.reshape(before.shape)
    whole[:, :, lane:] = after.reshape(before.shape)[:, :, : whole.shape[2] - lane]


def second_kernel(first, groups, held, voxels, homes, tiles, begin, end, *refs):
    rest = list(refs)
    owner, rows, foot, movie, mine, got = [rest.pop(0) for _ in range(6)]
    piece = rest.pop(0) if held < groups else None
    before = None if begin else (rest.pop(0), rest.pop(0))
    turned_before = None if begin else rest.pop(0)
    turned = rest.pop(0)
    after = [rest.pop(0)] if end else [rest.pop(0), rest.pop(0)]
    updated, crosses, grads = rest[:3]
    eye, block = masks()
    low_rows = lax.broadcasted_iota(jnp.int32, (16, lane), 0) < 8
    owners = owner[first : first + groups, :]
    total = mine[0:16, :] + got[0:16, :].astype(f32) + got[16:32, :].astype(f32)
    inverse = jnp.where(owners < homes * tiles, 1.0 / total[:groups], 0.0)
    for g in range(groups):
        at = slice(g * lane, (g + 1) * lane)
        scale = column(eye, inverse[g : g + 1, :])
        residual = mine[16 + g * lane : 16 + (g + 1) * lane, :]
        residual += got[head + g * lane : head + (g + 1) * lane, :].astype(f32)
        new = jnp.maximum(foot[at, :] + (residual - sparsity) * scale, 0.0)
        new = jnp.where(scale > 0.0, new, 0.0)
        updated[at, :] = new
    if begin:
        turn(updated, lax.axis_index("frame"), turned)
    else:
        second = rest[3]
        turn(updated, lax.axis_index("frame"), second)
        join_turned(turned_before, second, turned, first * lane // turned.shape[0])
    norms = []
    for g in range(groups):
        at = slice(g * lane, (g + 1) * lane)
        high, low = halves(updated[at, :])
        cross = dot(jnp.concatenate([high, low], 1), jnp.concatenate([high, high], 1), nt) + dot(high, low, nt)
        cross = jnp.where(block, cross, 0.0)
        norms.append(jnp.sum(jnp.where(eye, cross, 0.0), axis=0, keepdims=True))
        high, low = halves(cross)
        crosses[at, :lane] = high
        crosses[at, lane:] = low
    for g in range(groups):
        at = slice(g * lane, (g + 1) * lane)
        known = dot(crosses[at, :], jnp.concatenate([rows[at, :], rows[at, :]], 0))
        film, where = (movie, g * voxels) if g < held else (piece, (g - held) * voxels)
        for p in range(8):
            two = slice(where + p * 256, where + (p + 1) * 256)
            part = updated[g * lane + 16 * p : g * lane + 16 * p + 16, :]
            wide = jnp.concatenate([jnp.where(low_rows, part, 0.0), jnp.where(low_rows, 0.0, part)], 1)
            grad = dot(wide.astype(bf16), film[two, :]) - known[16 * p : 16 * p + 16]
            high, low = halves(grad)
            start = g * 2 * lane + 16 * p
            grads[start : start + 16, :] = high
            grads[start + lane : start + lane + 16, :] = low
    names = residents(lax.axis_index("tile"), homes, tiles, 0)
    trace_grad = jnp.zeros(after[0].shape, f32) if begin else before[0][...]
    weight = jnp.zeros(after[0].shape, f32) if begin else before[1][...]
    for g in range(groups):
        picks = owners[g : g + 1, :] == names
        onehot = picks.astype(f32).astype(bf16)
        trace_grad += dot(jnp.concatenate([onehot, onehot], 1), grads[g * 2 * lane : (g + 1) * 2 * lane, :])
        weight += jnp.where(picks, norms[g], 0.0)
    if end:
        step = trace_grad / jnp.maximum(jnp.sum(weight, axis=1, keepdims=True), 1.0)
        largest = jnp.maximum(jnp.max(jnp.abs(step), axis=(0, 1), keepdims=True), 1e-30)
        power = jnp.ceil(jnp.log2(largest * (1.0 / 32700.0)))
        whole = jnp.round(step * jnp.exp2(-power))
        spare = lax.rem(lax.broadcasted_iota(jnp.int32, step.shape, 0), 4) == 3
        after[0][...] = jnp.where(spare, power, whole).astype(jnp.int32).astype(jnp.int16)
    else:
        after[0][...] = trace_grad
        after[1][...] = weight


def local(movie, footprint, traces, slot_neuron, neuron_blocks):
    tiles, shares = lax.axis_size("tile"), lax.axis_size("frame")
    blocks, slots, width = footprint.shape
    homes, frames = traces.shape
    per_pair = homes // tiles
    slot_total = blocks * slots
    groups = slot_total // lane

    anywhere = pl.BlockSpec(memory_space=pl.ANY)
    vmem = pl.BlockSpec(memory_space=pltpu.VMEM)
    params = pltpu.CompilerParams(vmem_limit_bytes=32 * 1024 * 1024)

    def call(kernel, *static, **kw):
        return pl.pallas_call(lambda *refs: kernel(*static, *refs), compiler_params=params, **kw)

    def near(x):
        return pltpu.with_memory_space_constraint(x, pltpu.VMEM)

    def far(x):
        return pltpu.with_memory_space_constraint(x, pltpu.HBM)

    leaving = call(
        leaving_kernel,
        out_shape=pltpu.HBM((4 * tiles, frames), bf16),
        in_specs=[vmem],
        out_specs=vmem,
        scratch_shapes=[pltpu.VMEM((4 * tiles, frames), f32)],
    )(far(traces))
    recv = lax.all_to_all(leaving.reshape(tiles, 4, frames), "tile", 0, 0).reshape(4 * tiles, frames)

    foot = footprint.reshape(slot_total, width)

    voxels = movie.shape[0] // groups
    counts = [groups // 2, groups - groups // 2]
    firsts = [0, counts[0]]
    pieces = [counts[0], counts[1] - 1, 1]
    pairs = [[(s, s ^ 1) for s in range(shares)], [(s, shares - 1 - s) for s in range(shares)]]

    def exact_shape(c):
        return pltpu.VMEM((counts[c] * lane + 16, width), f32)

    def sent_shape(c):
        return pltpu.VMEM((counts[c] * lane + head, width), bf16)

    def film_shape(k):
        return pltpu.VMEM((pieces[k] * voxels, frames), bf16)

    film, owner = call(
        load_kernel,
        out_shape=(film_shape(0), pltpu.VMEM((groups, lane), jnp.int32)),
        in_specs=[anywhere, anywhere],
        out_specs=(vmem, vmem),
        scratch_shapes=[pltpu.VMEM((slots, blocks), jnp.int32), pltpu.SemaphoreType.DMA, pltpu.SemaphoreType.DMA],
        cost_estimate=pl.CostEstimate(flops=0, bytes_accessed=2 * movie.size, transcendentals=0),
    )(far(slot_neuron.T), far(movie))
    owner = near(owner)

    films, held, mine, got = [film], [], [], []
    for c in range(2):
        row, exact, sent, shapes, film = call(
            first_kernel,
            firsts[c],
            counts[c],
            pieces[c],
            voxels,
            homes,
            tiles,
            out_shape=(
                pltpu.VMEM((counts[c] * lane, frames), bf16),
                exact_shape(c),
                sent_shape(c),
                pltpu.VMEM((counts[c] * lane, width), f32),
                film_shape(c + 1),
            ),
            in_specs=[vmem, vmem, vmem, anywhere, anywhere],
            out_specs=(vmem,) * 5,
            scratch_shapes=[pltpu.VMEM((counts[c] * lane, 2 * lane), bf16)] + [pltpu.SemaphoreType.DMA] * 2,
        )(recv, owner, near(films[c]), far(foot), far(movie))
        films.append(film)
        held.append([row, shapes])
        mine.append(exact)
        got.append(lax.ppermute(sent, "frame", pairs[c]))
    for c in range(2):
        mine[c], sent = call(
            join_kernel, out_shape=(exact_shape(c), sent_shape(c)), in_specs=[vmem] * 2, out_specs=(vmem,) * 2
        )(near(mine[c]), near(got[c]))
        got[c] = lax.ppermute(sent, "frame", pairs[1 - c])

    kept, running = None, []
    for c in range(2):
        begin, end = c == 0, c == 1
        total_shape = (4 * tiles, frames)
        outs = [pltpu.VMEM((slots, width // shares, lane if begin else blocks), f32)]
        outs += [pltpu.VMEM(total_shape, jnp.int16)] if end else [pltpu.VMEM(total_shape, f32)] * 2
        more = [] if begin else [pltpu.VMEM((slots, width // shares, lane), f32)]
        old = [] if begin else [films[2]] + running + [kept]
        given = [*held[c], films[c], mine[c], got[c], *old]
        kept, *running = call(
            second_kernel,
            firsts[c],
            counts[c],
            pieces[c],
            voxels,
            homes,
            tiles,
            begin,
            end,
            out_shape=tuple(outs),
            in_specs=[vmem] * (1 + len(given)),
            out_specs=(vmem,) * len(outs),
            scratch_shapes=[
                pltpu.VMEM((counts[c] * lane, width), f32),
                pltpu.VMEM((counts[c] * lane, 2 * lane), bf16),
                pltpu.VMEM((2 * counts[c] * lane, frames), bf16),
            ]
            + more,
        )(owner, *[near(x) for x in given])
    ratio = running[0]

    back = lax.all_to_all(ratio.reshape(tiles, 4, frames), "tile", 0, 0)
    traces_new, kept = call(
        home_kernel,
        out_shape=(pltpu.HBM(traces.shape, f32), pltpu.HBM(kept.shape, f32)),
        in_specs=[vmem, vmem, vmem],
        out_specs=(anywhere, anywhere),
        scratch_shapes=[
            pltpu.VMEM((4 * tiles, frames), f32),
            pltpu.VMEM(traces.shape, f32),
            pltpu.SemaphoreType.DMA,
            pltpu.SemaphoreType.DMA,
        ],
    )(near(back.reshape(4 * tiles, frames)), near(traces), near(kept))
    return kept.transpose(2, 0, 1), traces_new


def solution(mesh):
    return jax.shard_map(
        local,
        mesh=mesh,
        in_specs=(
            P("tile", "frame"),
            P("tile", None, None),
            P("tile", "frame"),
            P("tile", None),
            P("tile", None),
        ),
        out_specs=(P("tile", None, "frame"), P("tile", "frame")),
        check_vma=False,
    )
```
